256 devices in a mesh: dp: 2 (over core), section: 4 (over x), tensor: 32 (over z, y).
Axes of the slice: x: 4, y: 4, z: 8, core: 2. Of those that a mesh axis runs over, the one named last changes fastest.
Arguments:
- hidden: bfloat16 [3, 4, 1024, 8192], P(None, 'section', ('dp', 'tensor')), parts along dimension 2, may hold values from -6 to 6
- exits: int32 [3, 1024], P(None, 'dp'), parts along dimension 1, may hold values from 0 to 2
- lengths: int32 [1024], P('dp'), parts along dimension 0, may hold values from 1 to 4092
- norm_gain: bfloat16 [4, 8192], P('section'), may hold values from 0.5 to 1.5
- w_key: bfloat16 [4, 2, 512, 8192], P('section', None, 'tensor'), may hold values from -0.0625 to 0.0625
- w_value: bfloat16 [4, 2, 512, 8192], P('section', None, 'tensor'), may hold values from -0.0625 to 0.0625
- w_query: bfloat16 [4, 2, 2048, 8192], P('section', None, 'tensor'), may hold values from -0.0625 to 0.0625
Outputs:
- new_keys: bfloat16 [3, 4, 2, 512, 1024], P(None, 'section', None, 'tensor', 'dp'), parts along dimension 4
- new_values: bfloat16 [3, 4, 2, 512, 1024], P(None, 'section', None, 'tensor', 'dp'), parts along dimension 4
- new_queries: bfloat16 [3, 4, 2, 2048, 1024], P(None, 'section', None, 'tensor', 'dp'), parts along dimension 4
The draws below stay inside these ranges and needn't reach their ends.
There are 2 independent parts, one for each index of `dp`. The reference program is written for one: setup_inputs(seed, part) draws one part's arguments, and reference() takes and returns one part's arrays. A program takes and returns all parts, laid end to end along the dimension named above; an argument that names none is the same for every part. Nothing has to cross between parts.
Inputs may be any that keep to these rules, and one draw needn't show every extreme that they name: 0: the row runs through all layers; 1: it exits after 4 // 4 layers; 2: after 4 // 2 layers.
All inputs are finite; a program needn't handle non-finite values.
Results may differ from the reference program's by a relative error of at most 0.0049.
Values may be sent and summed in bfloat16 or wider, within the bound.
No kernel may reach another device: no remote copies, remote signals or barrier semaphores. Data moves between devices by JAX's collectives and lax.ppermute only.
A program may use at most 128 MiB of HBM per device.

```python
import jax
import jax.numpy as jnp
from jax import lax

D = 8192
HEAD = 128
KVH = 8
QH = 32
STEPS = 3
CTX = 4096
ROWS = 512
LAYERS = 4


def with_ends(values, own_key, low, top_value):
    extent = values.shape
    index_at = [jax.random.randint(jax.random.fold_in(own_key, axis), (), 0, extent[axis]) for axis in range(len(extent))]
    values = values.at[tuple(index_at)].set(low)
    longest = extent.index(max(extent))
    index_at[longest] = (index_at[longest] + 1) % extent[longest]
    return values.at[tuple(index_at)].set(top_value)


def block_scale(stream_key, dims, shards, least, largest):
    level, own = 1.0, jax.random.fold_in(stream_key, 6)
    for dim, shards_of in shards:
        heights = jnp.exp(jax.random.uniform(jax.random.fold_in(own, dim), (shards_of,), jnp.float32, least / len(shards), largest / len(shards)))
        level = level * jnp.repeat(heights, dims[dim] // shards_of).reshape([-1 if axis == dim else 1 for axis in range(len(dims))])
    return level


def scatter_about(own_key, extent, deviation, limit, cuts=(), held_as=jnp.bfloat16):
    result = jax.random.normal(own_key, extent, jnp.float32) * deviation
    if len(cuts) > 0:
        result = block_scale(own_key, extent, cuts, -0.22, 0.18) * result
    return jnp.clip(result, min=-limit, max=limit).astype(held_as)


def setup_inputs(seed: int = 0, part: int = 0) -> dict:
    key_list = jax.random.split(jax.random.key(seed), 8)
    own_keys = jax.random.split(jax.random.fold_in(key_list[7], part), 8)
    return {
        "hidden": scatter_about(own_keys[0], (STEPS, LAYERS, ROWS, D), 1.0, 6.0, ((1, 4), (2, 32))),
        "exits": with_ends(jax.random.randint(own_keys[1], (STEPS, ROWS), 0, 3), jax.random.fold_in(own_keys[1], 1), 0, 2).astype(jnp.int32),
        "lengths": with_ends(jax.random.randint(own_keys[2], (ROWS,), 1, CTX - STEPS), jax.random.fold_in(own_keys[2], 1), 1, (CTX - STEPS) - 1).astype(jnp.int32),
        "norm_gain": jnp.clip(1.0 + 0.1 * jax.random.normal(key_list[3], (LAYERS, D), jnp.float32), 0.5, 1.5).astype(jnp.bfloat16),
        "w_key": scatter_about(key_list[4], (LAYERS, 2, KVH * HEAD // 2, D), D ** -0.5, 0.0625, ((0, 4), (2, 32))),
        "w_value": scatter_about(key_list[5], (LAYERS, 2, KVH * HEAD // 2, D), D ** -0.5, 0.0625, ((0, 4), (2, 32))),
        "w_query": scatter_about(key_list[6], (LAYERS, 2, QH * HEAD // 2, D), D ** -0.5, 0.0625, ((0, 4), (2, 32))),
    }


eps = 1e-05
theta = 10000.0

def rotate(pairs, positions, first, head):
    count = pairs.shape[1]
    index = ((jnp.arange(count, dtype=jnp.int32) + first) % (head // 2)).astype(jnp.float32)
    freqs = theta ** (-(index * 2.0) / head)
    angles = freqs[:, None] * positions.astype(jnp.float32)[None, :]
    cosine = jnp.cos(angles)
    sine = jnp.sin(angles)
    upper = pairs[0]
    lower = pairs[1]
    return jnp.stack([upper * cosine - lower * sine, lower * cosine + upper * sine], axis=0)

def apply_weight(weight, normed):
    dim = weight.shape[2]
    flat = weight.reshape(-1, dim)
    out = lax.dot_general(flat, normed, (((1,), (1,)), ((), ())), preferred_element_type=jnp.float32)
    return out.reshape(2, weight.shape[1], normed.shape[0])

def project(rows_in, gain, key_w, value_w, query_w, positions, first_kv, first_q, head):
    wide = rows_in.astype(jnp.float32)
    scale = lax.rsqrt(lax.optimization_barrier(jnp.mean(wide * wide, axis=-1, keepdims=True)) + eps)
    normed = (wide * scale * gain.astype(jnp.float32)).astype(jnp.bfloat16)
    keys = apply_weight(key_w, normed)
    values = apply_weight(value_w, normed)
    queries = apply_weight(query_w, normed)
    keys = rotate(keys, positions, first_kv, head)
    queries = rotate(queries, positions, first_q, head)
    return (keys.astype(jnp.bfloat16), values.astype(jnp.bfloat16), queries.astype(jnp.bfloat16))

def reference(hidden, exits, lengths, norm_gain, w_key, w_value, w_query):
    layers = hidden.shape[1]
    row_ids = jnp.arange(hidden.shape[2], dtype=jnp.int32)
    key_steps = []
    value_steps = []
    query_steps = []
    for step in range(STEPS):
        code = exits[step]
        depth = jnp.where(code == 1, layers // 4, jnp.where(code == 2, layers // 2, layers)).astype(jnp.int32)
        positions = (lengths + step).astype(jnp.int32)
        key_layers = []
        value_layers = []
        query_layers = []
        for layer in range(layers):
            source = jnp.minimum(depth, layer).astype(jnp.int32)
            chosen = hidden[step][source, row_ids]
            keys, values, queries = project(chosen, norm_gain[layer], w_key[layer], w_value[layer], w_query[layer], positions, 0, 0, HEAD)
            key_layers.append(keys)
            value_layers.append(values)
            query_layers.append(queries)
        key_steps.append(jnp.stack(key_layers))
        value_steps.append(jnp.stack(value_layers))
        query_steps.append(jnp.stack(query_layers))
    return (jnp.stack(key_steps), jnp.stack(value_steps), jnp.stack(query_steps))
```

```python
import functools

import jax
import jax.numpy as jnp
from jax import lax
from jax.experimental import pallas as pl
from jax.experimental.pallas import tpu as pltpu
from jax.sharding import PartitionSpec as P

HEAD = 128
EPS = 1e-05
THETA = 10000.0

STEPS = 3
DIM = 8192
HALF = DIM // 2
QUARTER = DIM // 4
SHARD = 16
NZ = 8
NY = 4
KV = 16
Q = 64
COLS = 4 * KV + 2 * Q
LANES = NZ * SHARD
KC = 1024
VMEM_LIMIT = 48 * 1024 * 1024

CHUNKS = ((0, 1), (1, 2), (2, 3))


def shift_z(value, by):
    pairs = [(z * NY + y, ((z + by) % NZ) * NY + y) for z in range(NZ) for y in range(NY)]
    return lax.ppermute(value, "tensor", pairs)


def shift_y(value, by):
    pairs = [(z * NY + y, z * NY + (y + by) % NY) for z in range(NZ) for y in range(NY)]
    return lax.ppermute(value, "tensor", pairs)


def swap_cores(value):
    return lax.ppermute(value, "dp", [(0, 1), (1, 0)])


def norm_kernel(core_ref, own_ref, one_ref, two_ref, back_ref, gain_ref, out_ref):
    back = back_ref[0]
    wide = jnp.where(
        back == 2,
        two_ref[0].astype(jnp.float32),
        jnp.where(back == 1, one_ref[0].astype(jnp.float32), own_ref[0].astype(jnp.float32)),
    )
    scale = lax.rsqrt(jnp.mean(wide * wide, axis=-1, keepdims=True) + EPS)
    normed = (wide * scale * gain_ref[...].astype(jnp.float32)).astype(jnp.bfloat16)
    low = normed[:, :HALF]
    high = normed[:, HALF:]

    @pl.when(core_ref[0] == 0)
    def _():
        out_ref[0, 0] = low
        out_ref[1, 0] = high

    @pl.when(core_ref[0] != 0)
    def _():
        out_ref[0, 0] = high
        out_ref[1, 0] = low


def norm_rows(core, own, one, two, back, gain):
    steps = own.shape[0]
    rows = pl.BlockSpec((1, SHARD, DIM), lambda t, c: (t, 0, 0))
    return pl.pallas_call(
        norm_kernel,
        out_shape=jax.ShapeDtypeStruct((2, steps, SHARD, HALF), jnp.bfloat16),
        grid_spec=pltpu.PrefetchScalarGridSpec(
            num_scalar_prefetch=1,
            grid=(steps,),
            in_specs=[
                rows,
                rows,
                rows,
                pl.BlockSpec((1, SHARD, 1), lambda t, c: (t, 0, 0)),
                pl.BlockSpec((1, DIM), lambda t, c: (0, 0)),
            ],
            out_specs=pl.BlockSpec((2, 1, SHARD, HALF), lambda t, c: (0, t, 0, 0)),
        ),
        compiler_params=pltpu.CompilerParams(vmem_limit_bytes=VMEM_LIMIT),
        cost_estimate=pl.CostEstimate(
            flops=6 * steps * SHARD * DIM, bytes_accessed=8 * steps * SHARD * DIM, transcendentals=0
        ),
    )(core, own, one, two, back, gain)


def project_kernel(steps, place_ref, *refs):
    wk, wv, wq = refs[0:3]
    left, left_far, right, right_far = refs[3:7]
    across = refs[7:11]
    acts = refs[11:18]
    act_low, act_high = refs[18:20]
    cos_ref, sin_ref = refs[20:22]
    outs = refs[22:26]
    total = refs[26]
    k = pl.program_id(0)

    @pl.when(k == 0)
    def _():
        total[...] = jnp.zeros_like(total)

    per_half = HALF // KC
    for quarter in range(4):

        @pl.when(k // (per_half // 2) == quarter)
        def _(quarter=quarter):
            near = quarter < 2
            weights = [
                wk[0].reshape(2 * KV, KC),
                wv[0].reshape(2 * KV, KC),
                wq[0].reshape(2 * Q, KC),
                (left if near else left_far)[0],
                (right if near else right_far)[0],
                across[quarter][...],
            ]
            weight = jnp.concatenate(weights, axis=0)
            opposite = act_low if near else act_high
            rows = []
            for t in range(steps):
                for d in range(NZ):
                    if d < 4:
                        rows.append(acts[d][0, t])
                    elif d == 4:
                        rows.append(opposite[t])
                    else:
                        rows.append(acts[d - 1][0, t])
            act = jnp.concatenate(rows, axis=0)
            total[...] += lax.dot_general(
                weight, act, (((1,), (1,)), ((), ())), preferred_element_type=jnp.float32
            )

    @pl.when(k == pl.num_programs(0) - 1)
    def _():
        y = place_ref[1]
        for block, by in enumerate((0, 3, 1, 2)):
            first = block * COLS
            source = lax.rem(y + by, NY)
            kv_rows = pl.ds(pl.multiple_of(source * KV, KV), KV)
            for t in range(steps):
                lanes = slice(t * LANES, (t + 1) * LANES)

                def part(offset, count):
                    return total[first + offset : first + offset + count, lanes]

                def put(offset, count, value):
                    outs[block][t, offset : offset + count, :] = value.astype(jnp.bfloat16)

                a, b = part(0, KV), part(KV, KV)
                cosine, sine = cos_ref[kv_rows, lanes], sin_ref[kv_rows, lanes]
                put(0, KV, a * cosine - b * sine)
                put(KV, KV, b * cosine + a * sine)
                put(2 * KV, 2 * KV, part(2 * KV, 2 * KV))
                a, b = part(4 * KV, Q), part(4 * KV + Q, Q)
                cosine, sine = cos_ref[:, lanes], sin_ref[:, lanes]
                put(4 * KV, Q, a * cosine - b * sine)
                put(4 * KV + Q, Q, b * cosine + a * sine)


def project(steps, place, weights, left, left_far, right, right_far, across, acts, act_low, act_high, cosine, sine):
    per_half = HALF // KC
    per_quarter = per_half // 2

    def own_weight(rows):
        return pl.BlockSpec(
            (1, 2, rows, KC), lambda k, p: (0, 0, 0, lax.rem(p[0] * per_half + k, 2 * per_half))
        )

    def clip(value, top):
        return jnp.minimum(jnp.maximum(value, 0), top)

    def side(first):
        def index(k, p):
            at = clip(k - first, per_half - 1)
            return at // per_quarter, 0, at % per_quarter

        return pl.BlockSpec((1, COLS, KC), index)

    def far(quarter):
        return pl.BlockSpec(
            (COLS, KC), lambda k, p: (0, clip(k - quarter * per_quarter, per_quarter - 1))
        )

    def opposite(first):
        return pl.BlockSpec(
            (steps, SHARD, KC), lambda k, p: (0, 0, clip(k - first, per_half - 1))
        )

    act = pl.BlockSpec((1, steps, SHARD, KC), lambda k, p: (k // per_half, 0, 0, k % per_half))
    table = pl.BlockSpec((HEAD // 2, steps * LANES), lambda k, p: (0, 0))
    out = pl.BlockSpec((steps, COLS, LANES), lambda k, p: (0, 0, 0))
    return pl.pallas_call(
        functools.partial(project_kernel, steps),
        out_shape=[jax.ShapeDtypeStruct((steps, COLS, LANES), jnp.bfloat16)] * 4,
        grid_spec=pltpu.PrefetchScalarGridSpec(
            num_scalar_prefetch=1,
            grid=(2 * per_half,),
            in_specs=[own_weight(KV), own_weight(KV), own_weight(Q)]
            + [side(0), side(per_half), side(0), side(per_half)]
            + [far(quarter) for quarter in range(4)]
            + [act] * 7
            + [opposite(0), opposite(per_half)]
            + [table, table],
            out_specs=[out] * 4,
            scratch_shapes=[pltpu.VMEM((4 * COLS, steps * LANES), jnp.float32)],
        ),
        compiler_params=pltpu.CompilerParams(vmem_limit_bytes=VMEM_LIMIT),
        cost_estimate=pl.CostEstimate(
            flops=2 * 4 * COLS * DIM * steps * LANES,
            bytes_accessed=2 * DIM * (4 * COLS + steps * LANES),
            transcendentals=0,
        ),
    )(place, *weights, left, left_far, right, right_far, *across, *acts, act_low, act_high, cosine, sine)


def place_kernel(sizes, place_ref, *refs):
    pieces = refs[: 4 * len(sizes)]
    keys, values, queries = refs[4 * len(sizes) :]
    y, z = place_ref[1], place_ref[2]
    width = NZ * NY * SHARD
    lane = lax.broadcasted_iota(jnp.int32, (LANES, width), 0)
    target = lax.broadcasted_iota(jnp.int32, (LANES, width), 1)
    plane = lax.rem(z + NZ - lane // SHARD, NZ)
    chosen = []
    for by in (0, 1, 3, 2):
        at = plane * (NY * SHARD) + lax.rem(y + by, NY) * SHARD + lane % SHARD
        chosen.append(jnp.where(at == target, 1.0, 0.0).astype(jnp.bfloat16))
    step = 0
    for group, size in enumerate(sizes):
        for t in range(size):
            full = jnp.zeros((COLS, width), jnp.float32)
            for block in range(4):
                full += jnp.dot(
                    pieces[4 * group + block][t], chosen[block], preferred_element_type=jnp.float32
                )
            full = full.astype(jnp.bfloat16)
            keys[step, 0] = full[: 2 * KV].reshape(2, KV, width)
            values[step, 0] = full[2 * KV : 4 * KV].reshape(2, KV, width)
            queries[step, 0] = full[4 * KV :].reshape(2, Q, width)
            step += 1


def place_outputs(sizes, place, pieces):
    width = NZ * NY * SHARD
    whole = pl.BlockSpec(memory_space=pltpu.VMEM)
    return pl.pallas_call(
        functools.partial(place_kernel, sizes),
        out_shape=[
            jax.ShapeDtypeStruct((STEPS, 1, 2, KV, width), jnp.bfloat16),
            jax.ShapeDtypeStruct((STEPS, 1, 2, KV, width), jnp.bfloat16),
            jax.ShapeDtypeStruct((STEPS, 1, 2, Q, width), jnp.bfloat16),
        ],
        in_specs=[pl.BlockSpec(memory_space=pltpu.SMEM)] + [whole] * len(pieces),
        out_specs=[whole] * 3,
        compiler_params=pltpu.CompilerParams(vmem_limit_bytes=VMEM_LIMIT),
    )(place, *pieces)


def on_device(hidden, exits, lengths, norm_gain, w_key, w_value, w_query):
    core = lax.axis_index("dp").astype(jnp.int32)
    layer = lax.axis_index("section").astype(jnp.int32)
    index = lax.axis_index("tensor").astype(jnp.int32)
    z, y = index // NY, index % NY
    place = jnp.stack([core, y, z])

    flat = jnp.concatenate(
        [w_key.reshape(2 * KV, DIM), w_value.reshape(2 * KV, DIM), w_query.reshape(2 * Q, DIM)], axis=0
    )
    half = lax.dynamic_slice_in_dim(flat, core * HALF, HALF, axis=1)
    half = half.reshape(COLS, 2, QUARTER).transpose(1, 0, 2)
    left = shift_y(half, 1)
    right = shift_y(half, -1)
    far_low = shift_y(left[0], 1)
    far_high = shift_y(right[1], -1)
    left_far = swap_cores(left)
    right_far = swap_cores(right)
    across = (far_low, far_high, swap_cores(far_low), swap_cores(far_high))

    delta = jnp.arange(NZ, dtype=jnp.int32)
    rows = ((z + NZ - delta) % NZ)[:, None] * (NY * SHARD) + y * SHARD
    rows = (rows + jnp.arange(SHARD, dtype=jnp.int32)[None, :]).reshape(LANES)
    everyone = jnp.arange(lengths.shape[0], dtype=jnp.int32)
    mine = jnp.sum(jnp.where(rows[:, None] == everyone[None, :], lengths[None, :], 0), axis=1)
    pair = jnp.arange(HEAD // 2, dtype=jnp.int32).astype(jnp.float32)
    freqs = THETA ** (-(pair * 2.0) / HEAD)
    positions = (mine[None, :] + jnp.arange(STEPS, dtype=jnp.int32)[:, None]).reshape(-1)
    angles = freqs[:, None] * positions.astype(jnp.float32)[None, :]
    cosine, sine = jnp.cos(angles), jnp.sin(angles)

    code = lax.dynamic_slice_in_dim(exits, index * SHARD, SHARD, axis=1)
    depth = jnp.where(code == 1, 1, jnp.where(code == 2, 2, 4))
    back = (layer - jnp.minimum(depth, layer))[:, :, None]

    pieces = []
    for first, last in CHUNKS:
        steps = last - first
        own = hidden[first:last, 0]
        one = lax.ppermute(own, "section", [(1, 2), (2, 3)])
        two = lax.ppermute(own, "section", [(1, 3)])
        mine = norm_rows(core[None], own, one, two, back[first:last], norm_gain)
        up = [mine]
        down = [mine]
        for _ in range(3):
            up.append(shift_z(up[-1], 1))
            down.append(shift_z(down[-1], -1))
        act_low = shift_z(up[3][0], 1)
        act_high = shift_z(down[3][1], -1)
        acts = up + down[:0:-1]
        lanes = slice(first * LANES, last * LANES)
        outs = project(
            steps,
            place,
            (w_key, w_value, w_query),
            left,
            left_far,
            right,
            right_far,
            across,
            acts,
            act_low,
            act_high,
            cosine[:, lanes],
            sine[:, lanes],
        )
        pieces.extend([outs[0], shift_y(outs[1], -1), shift_y(outs[2], 1), shift_y(outs[3], 2)])
    return tuple(place_outputs(tuple(b - a for a, b in CHUNKS), place, pieces))


def solution(mesh):
    return jax.shard_map(
        on_device,
        mesh=mesh,
        in_specs=(
            P(None, "section", ("dp", "tensor"), None),
            P(None, "dp"),
            P("dp"),
            P("section", None),
            P("section", None, "tensor", None),
            P("section", None, "tensor", None),
            P("section", None, "tensor", None),
        ),
        out_specs=(
            P(None, "section", None, "tensor", "dp"),
            P(None, "section", None, "tensor", "dp"),
            P(None, "section", None, "tensor", "dp"),
        ),
        check_vma=False,
    )
```

```python
import functools

import jax
import jax.numpy as jnp
from jax import lax
from jax.experimental import pallas as pl
from jax.experimental.pallas import tpu as pltpu
from jax.sharding import PartitionSpec as P

HEAD = 128
EPS = 1e-05
THETA = 10000.0

STEPS = 3
DIM = 8192
HALF = DIM // 2
SHARD = 16
NZ = 8
NY = 4
KV = 16
Q = 64
SIDE = Q + 2 * KV
COLS = 2 * SIDE
ROWS = STEPS * SHARD
LANES = NZ * SHARD
PARTS = 2
PART = DIM // PARTS
MEBI = 1024 * 1024
VMEM_PROJECT = 16 * MEBI
EXTRA = 128
CHUNK = 512
WEIGHT_GROUPS = [
    [core * NZ * NY + z * NY + y for y in range(NY) for core in range(2)] for z in range(NZ)
]


def shift_z(value, by):
    pairs = [(z * NY + y, ((z + by) % NZ) * NY + y) for z in range(NZ) for y in range(NY)]
    return lax.ppermute(value, "tensor", pairs)


def shift_y(value, by):
    pairs = [(z * NY + y, z * NY + (y + by) % NY) for z in range(NZ) for y in range(NY)]
    return lax.ppermute(value, "tensor", pairs)


def copies(pairs, sems):
    started = []
    for i, (source, target) in enumerate(pairs):
        copy = pltpu.make_async_copy(source, target, sems.at[i])
        copy.start()
        started.append(copy)
    return started


def fetch_kernel(*refs):
    weight_ref, low_refs, high_refs = refs[0], refs[1:NZ], refs[NZ : 2 * NZ - 1]
    weight_out, low_out, high_out, sems = refs[2 * NZ - 1 :]
    pairs = [(weight_ref.at[:, at], weight_out.at[:, at]) for at in (slice(0, HALF), slice(HALF, DIM))]
    pairs += [(ref, low_out.at[i]) for i, ref in enumerate(low_refs)]
    pairs += [(ref, high_out.at[i]) for i, ref in enumerate(high_refs)]
    for copy in copies(pairs, sems):
        copy.wait()


def fetch(weight, low, high):
    operands = [pltpu.with_memory_space_constraint(x, pltpu.HBM) for x in (weight, *low, *high)]
    shapes = [
        weight.shape,
        (NZ - 1, ROWS, HALF),
        (NZ - 1, ROWS, HALF + EXTRA),
    ]
    return pl.pallas_call(
        fetch_kernel,
        out_shape=[jax.ShapeDtypeStruct(shape, jnp.bfloat16) for shape in shapes],
        in_specs=[pl.BlockSpec(memory_space=pltpu.HBM)] * len(operands),
        out_specs=[pl.BlockSpec(memory_space=pltpu.VMEM)] * 3,
        scratch_shapes=[pltpu.SemaphoreType.DMA((2 * NZ,))],
        compiler_params=pltpu.CompilerParams(vmem_limit_bytes=VMEM_PROJECT),
        cost_estimate=pl.CostEstimate(
            flops=0, bytes_accessed=2 * DIM * (NY * COLS + 2 * NZ * ROWS), transcendentals=0
        ),
    )(*operands)


def weigh_kernel(first, own_ref, one_ref, two_ref, back_ref, gain_ref, *refs):
    out_ref = refs[0] if first else refs[1]
    for t in range(STEPS):
        rows = slice(t * SHARD, (t + 1) * SHARD)
        back = back_ref[rows]
        squares = jnp.zeros((SHARD, CHUNK), jnp.float32)
        for start in range(0, HALF, CHUNK):
            at = slice(start, start + CHUNK)
            own, one, two = (ref[rows, at].astype(jnp.float32) for ref in (own_ref, one_ref, two_ref))
            wide = jnp.where(back == 2, two, jnp.where(back == 1, one, own))
            squares += wide * wide
            out_ref[rows, at] = (wide * gain_ref[:, at].astype(jnp.float32)).astype(jnp.bfloat16)
        square = jnp.sum(squares, axis=-1, keepdims=True)
        if first:
            refs[1][rows] = square
            continue
        rest = lax.rsqrt((refs[0][rows] + square) / DIM + EPS)
        lane = lax.broadcasted_iota(jnp.int32, (SHARD, EXTRA), 1)
        tail = jnp.zeros((SHARD, EXTRA), jnp.float32)
        for i in range(3):
            term = rest.astype(jnp.bfloat16).astype(jnp.float32)
            tail = jnp.where(lane == i, term, tail)
            rest = rest - term
        out_ref[rows, HALF:] = tail.astype(jnp.bfloat16)


def weigh_rows(states, back, gain, earlier):
    whole = pl.BlockSpec(memory_space=pltpu.VMEM)
    first = earlier is None
    out_shape = [jax.ShapeDtypeStruct((ROWS, HALF + (0 if first else EXTRA)), jnp.bfloat16)]
    if first:
        out_shape.append(jax.ShapeDtypeStruct((ROWS, 1), jnp.float32))
    operands = [*states, back, gain] + ([] if first else [earlier])
    return pl.pallas_call(
        functools.partial(weigh_kernel, first),
        out_shape=out_shape,
        in_specs=[whole] * len(operands),
        out_specs=[whole] * len(out_shape),
        compiler_params=pltpu.CompilerParams(vmem_limit_bytes=16 * MEBI),
        cost_estimate=pl.CostEstimate(
            flops=6 * ROWS * HALF, bytes_accessed=8 * ROWS * HALF, transcendentals=0
        ),
    )(*operands)


def project_kernel(half, place_ref, weight_ref, near_ref, far_ref, *refs):
    far, sems = refs[-2:]

    waiting = []
    for part in range(HALF // PART):
        last = half == 1 and part == HALF // PART - 1
        at = slice(part * PART, (part + 1) * PART + (EXTRA if last else 0))
        waiting.append(copies([(far_ref.at[:, at], far.at[:, at])], sems.at[part : part + 1]))

    def piece(d, rows, columns):
        if d == 4:
            return far[rows, columns]
        return near_ref[d if d < 4 else d - 1, rows, columns]

    def in_order(first, width):
        rows = []
        for t in range(STEPS):
            at = slice(t * SHARD, (t + 1) * SHARD)
            rows += [piece(d, at, slice(first, first + width)) for d in range(NZ)]
        return jnp.concatenate(rows, axis=0)

    def multiply(part):
        for copy in waiting[part]:
            copy.wait()
        first = part * PART
        return lax.dot_general(
            weight_ref[:, half * HALF + first : half * HALF + first + PART],
            in_order(first, PART),
            (((1,), (1,)), ((), ())),
            preferred_element_type=jnp.float32,
        )

    if half == 0:
        total = refs[0]
        total[...] = multiply(0)
        for part in range(1, HALF // PART):
            total[...] += multiply(part)
        return

    carried, cos_ref, sin_ref, *outs, total = refs[:-2]
    total[...] = carried[...] + multiply(0)
    for part in range(1, HALF // PART):
        total[...] += multiply(part)
    y = place_ref[1]
    ones = jnp.where(lax.broadcasted_iota(jnp.int32, (8, EXTRA), 1) < 3, 1.0, 0.0)
    scale = lax.dot_general(
        ones.astype(jnp.bfloat16),
        in_order(HALF, EXTRA),
        (((1,), (1,)), ((), ())),
        preferred_element_type=jnp.float32,
    )[0:1]

    for by in range(NY):
        to = lax.rem(y + by, NY)
        kv_rows = pl.ds(pl.multiple_of(to * KV, KV), KV)
        low = to * COLS
        high = low + SIDE

        def part(base, offset, rows):
            return total[pl.ds(pl.multiple_of(base + offset, KV), rows), :] * scale

        def put(offset, value):
            outs[by][offset : offset + value.shape[0], :] = value.astype(jnp.bfloat16)

        a, b = part(low, Q, KV), part(high, Q, KV)
        cosine, sine = cos_ref[kv_rows, :], sin_ref[kv_rows, :]
        put(0, a * cosine - b * sine)
        put(KV, b * cosine + a * sine)
        put(2 * KV, part(low, Q + KV, KV))
        put(3 * KV, part(high, Q + KV, KV))
        a, b = part(low, 0, Q), part(high, 0, Q)
        cosine, sine = cos_ref[...], sin_ref[...]
        put(4 * KV, a * cosine - b * sine)
        put(4 * KV + Q, b * cosine + a * sine)


def project(place, weight, half, near, far, local=()):
    lanes = STEPS * LANES
    whole = pl.BlockSpec(memory_space=pltpu.VMEM)
    total = (NY * COLS, lanes)
    scratch = [
        pltpu.VMEM(far.shape, jnp.bfloat16),
        pltpu.SemaphoreType.DMA((HALF // PART,)),
    ]
    if half == 0:
        out_shape = [jax.ShapeDtypeStruct(total, jnp.float32)]
    else:
        out_shape = [jax.ShapeDtypeStruct((COLS, lanes), jnp.bfloat16)] * NY
        scratch = [pltpu.VMEM(total, jnp.float32)] + scratch
    return pl.pallas_call(
        functools.partial(project_kernel, half),
        out_shape=out_shape,
        in_specs=[pl.BlockSpec(memory_space=pltpu.SMEM), whole, whole]
        + [pl.BlockSpec(memory_space=pltpu.HBM)]
        + [whole] * len(local),
        out_specs=[whole] * len(out_shape),
        scratch_shapes=scratch,
        compiler_params=pltpu.CompilerParams(vmem_limit_bytes=VMEM_PROJECT),
        cost_estimate=pl.CostEstimate(
            flops=2 * NY * COLS * HALF * lanes,
            bytes_accessed=4 * HALF * (NY * COLS + lanes),
            transcendentals=0,
        ),
    )(place, weight, near, pltpu.with_memory_space_constraint(far, pltpu.HBM), *local)


def place_kernel(place_ref, *refs):
    pieces, (keys, values, queries) = refs[:NY], refs[NY:]
    y, z = place_ref[1], place_ref[2]
    width = NZ * NY * SHARD
    lane = lax.broadcasted_iota(jnp.int32, (LANES, 1), 0)
    column = lax.broadcasted_iota(jnp.int32, (LANES, width), 1)
    plane = lax.rem(z + NZ - lane // SHARD, NZ)
    chosen = []
    for by in range(NY):
        source = lax.rem(y + NY - by, NY)
        at = plane * (NY * SHARD) + source * SHARD + lane % SHARD
        chosen.append(jnp.where(at == column, 1.0, 0.0).astype(jnp.bfloat16))
    chosen = jnp.concatenate(chosen, axis=0)
    for t in range(STEPS):
        lanes = slice(t * LANES, (t + 1) * LANES)
        rows = [ref[:, lanes] for ref in pieces]
        full = jnp.dot(
            jnp.concatenate(rows, axis=1), chosen, preferred_element_type=jnp.float32
        ).astype(jnp.bfloat16)
        keys[t, 0] = full[: 2 * KV].reshape(2, KV, width)
        values[t, 0] = full[2 * KV : 4 * KV].reshape(2, KV, width)
        queries[t, 0] = full[4 * KV :].reshape(2, Q, width)


def place_outputs(place, pieces):
    width = NZ * NY * SHARD
    whole = pl.BlockSpec(memory_space=pltpu.VMEM)
    return pl.pallas_call(
        place_kernel,
        out_shape=[
            jax.ShapeDtypeStruct((STEPS, 1, 2, KV, width), jnp.bfloat16),
            jax.ShapeDtypeStruct((STEPS, 1, 2, KV, width), jnp.bfloat16),
            jax.ShapeDtypeStruct((STEPS, 1, 2, Q, width), jnp.bfloat16),
        ],
        in_specs=[pl.BlockSpec(memory_space=pltpu.SMEM)] + [whole] * len(pieces),
        out_specs=[whole] * 3,
        compiler_params=pltpu.CompilerParams(vmem_limit_bytes=16 * MEBI),
    )(place, *pieces)


def after(value, *earlier):
    return lax.optimization_barrier((value, *earlier))[0]


def on_device(hidden, exits, lengths, norm_gain, w_key, w_value, w_query):
    core = lax.axis_index("dp").astype(jnp.int32)
    layer = lax.axis_index("section").astype(jnp.int32)
    index = lax.axis_index("tensor").astype(jnp.int32)
    z, y = index // NY, index % NY
    place = jnp.stack([core, y, z])

    code = lax.dynamic_slice_in_dim(exits, index * SHARD, SHARD, axis=1)
    depth = jnp.where(code == 1, 1, jnp.where(code == 2, 2, 4))
    back = (layer - jnp.minimum(depth, layer)).reshape(ROWS, 1)

    everyone = jnp.arange(lengths.shape[0], dtype=jnp.int32)
    pair = jnp.arange(HEAD // 2, dtype=jnp.int32).astype(jnp.float32)
    freqs = THETA ** (-(pair * 2.0) / HEAD)

    def tables(planes):
        delta = jnp.array(list(planes), dtype=jnp.int32)
        rows = ((z + NZ - delta) % NZ) * (NY * SHARD) + y * SHARD
        rows = (rows[:, None] + jnp.arange(SHARD, dtype=jnp.int32)[None, :]).reshape(-1)
        mine = jnp.sum(jnp.where(rows[:, None] == everyone[None, :], lengths[None, :], 0), axis=1)
        positions = mine[None, :] + jnp.arange(STEPS, dtype=jnp.int32)[:, None]
        angles = freqs[:, None] * positions.reshape(-1).astype(jnp.float32)[None, :]
        return jnp.cos(angles), jnp.sin(angles)

    own = hidden.reshape(ROWS, DIM)
    moved = []
    for half in range(2):
        mine = own[:, half * HALF : (half + 1) * HALF]
        one = lax.ppermute(mine, "section", [(1, 2), (2, 3)])
        two = lax.ppermute(mine, "section", [(1, 3)])
        moved.append((mine, one, two))
    def half_of(w):
        return lax.dynamic_index_in_dim(w[0], core, axis=0, keepdims=False)

    w_query, w_key, w_value, _ = lax.optimization_barrier((w_query, w_key, w_value, moved[0][0]))
    half = jnp.concatenate([half_of(w_query), half_of(w_key), half_of(w_value)], axis=0)
    weight = lax.all_gather(
        half, ("dp", "tensor"), axis_index_groups=WEIGHT_GROUPS, tiled=True
    )

    low, square = weigh_rows(moved[0], back, norm_gain[:, :HALF], None)
    (high,) = weigh_rows(moved[1], back, norm_gain[:, HALF:], square)

    chains = []
    for half, rows in enumerate((low, high)):
        up, down = [rows], [rows]
        for _ in range(3):
            here = lax.optimization_barrier((up[-1], down[-1]))
            up.append(shift_z(here[0], 1))
            down.append(shift_z(here[1], -1))
        here = lax.optimization_barrier((up[-1], down[-1]))
        last = shift_z(after(here[half], weight) if half else here[half], 1 - 2 * half)
        chains.append(up + [last] + down[:0:-1])

    low, high = chains
    weight, low_near, high_near = fetch(weight, low[:4] + low[5:], high[:4] + high[5:])
    (carried,) = project(place, weight, 0, low_near, low[4])
    outs = project(place, weight, 1, high_near, high[4], (carried, *tables(range(NZ))))
    pieces = [outs[0], shift_y(outs[1], 1), shift_y(outs[2], 2), shift_y(outs[3], -1)]
    return tuple(place_outputs(place, pieces))


def solution(mesh):
    return jax.shard_map(
        on_device,
        mesh=mesh,
        in_specs=(
            P(None, "section", ("dp", "tensor"), None),
            P(None, "dp"),
            P("dp"),
            P("section", None),
            P("section", None, "tensor", None),
            P("section", None, "tensor", None),
            P("section", None, "tensor", None),
        ),
        out_specs=(
            P(None, "section", None, "tensor", "dp"),
            P(None, "section", None, "tensor", "dp"),
            P(None, "section", None, "tensor", "dp"),
        ),
        check_vma=False,
    )
```

```python
import functools

import jax
import jax.numpy as jnp
from jax import lax
from jax.experimental import pallas as pl
from jax.experimental.pallas import tpu as pltpu
from jax.sharding import PartitionSpec as P

HEAD = 128
EPS = 1e-05
THETA = 10000.0

STEPS = 3
DIM = 8192
HALF = DIM // 2
SHARD = 16
NZ = 8
NY = 4
KV = 16
Q = 64
SIDE = Q + 2 * KV
COLS = 2 * SIDE
ROWS = STEPS * SHARD
LANES = NZ * SHARD
PARTS = 2
PART = DIM // PARTS
MEBI = 1024 * 1024
VMEM_PROJECT = 16 * MEBI
EXTRA = 128
ORDER = (0, 1, 2, 3, 5, 6, 7, 4)
CHUNK = 512
WEIGHT_GROUPS = [
    [core * NZ * NY + z * NY + y for y in range(NY) for core in range(2)] for z in range(NZ)
]


def shift_z(value, by):
    pairs = [(z * NY + y, ((z + by) % NZ) * NY + y) for z in range(NZ) for y in range(NY)]
    return lax.ppermute(value, "tensor", pairs)


def shift_y(value, by):
    pairs = [(z * NY + y, z * NY + (y + by) % NY) for z in range(NZ) for y in range(NY)]
    return lax.ppermute(value, "tensor", pairs)


def copies(pairs, sems):
    started = []
    for i, (source, target) in enumerate(pairs):
        copy = pltpu.make_async_copy(source, target, sems.at[i])
        copy.start()
        started.append(copy)
    return started


def split_kernel(place_ref, rows_ref, query_ref, key_ref, value_ref, low_ref, high_ref, half_ref):
    k = pl.program_id(0)
    steps = pl.num_programs(0) // 2

    @pl.when(k < steps)
    def _():
        low_ref[...] = rows_ref[...]

    @pl.when(k >= steps)
    def _():
        high_ref[...] = rows_ref[...]

    half_ref[:Q] = query_ref[0, 0]
    half_ref[Q : Q + KV] = key_ref[0, 0]
    half_ref[Q + KV :] = value_ref[0, 0]


def split(place, rows, query, key, value):
    steps = HALF // PART

    def mine(count):
        return pl.BlockSpec((1, 1, count, PART), lambda k, p: (0, p[0], 0, k))

    return pl.pallas_call(
        split_kernel,
        out_shape=[
            jax.ShapeDtypeStruct((ROWS, HALF), jnp.bfloat16),
            jax.ShapeDtypeStruct((ROWS, HALF), jnp.bfloat16),
            jax.ShapeDtypeStruct((SIDE, DIM), jnp.bfloat16),
        ],
        grid_spec=pltpu.PrefetchScalarGridSpec(
            num_scalar_prefetch=1,
            grid=(2 * steps,),
            in_specs=[
                pl.BlockSpec((ROWS, PART), lambda k, p: (0, k)),
                mine(Q),
                mine(KV),
                mine(KV),
            ],
            out_specs=[
                pl.BlockSpec((ROWS, PART), lambda k, p: (0, jnp.minimum(k, steps - 1))),
                pl.BlockSpec((ROWS, PART), lambda k, p: (0, jnp.maximum(k - steps, 0))),
                pl.BlockSpec((SIDE, PART), lambda k, p: (0, k)),
            ],
        ),
        compiler_params=pltpu.CompilerParams(vmem_limit_bytes=16 * MEBI),
        cost_estimate=pl.CostEstimate(
            flops=0, bytes_accessed=4 * (ROWS + SIDE) * DIM, transcendentals=0
        ),
    )(place, *(pltpu.with_memory_space_constraint(x, pltpu.HBM) for x in (rows, query, key, value)))


def weigh_kernel(first, own_ref, one_ref, two_ref, back_ref, gain_ref, *refs):
    out_ref = refs[0] if first else refs[1]
    for t in range(STEPS):
        rows = slice(t * SHARD, (t + 1) * SHARD)
        back = back_ref[rows]
        squares = jnp.zeros((SHARD, CHUNK), jnp.float32)
        for start in range(0, HALF, CHUNK):
            at = slice(start, start + CHUNK)
            own, one, two = (ref[rows, at].astype(jnp.float32) for ref in (own_ref, one_ref, two_ref))
            wide = jnp.where(back == 2, two, jnp.where(back == 1, one, own))
            squares += wide * wide
            out_ref[rows, at] = (wide * gain_ref[:, at].astype(jnp.float32)).astype(jnp.bfloat16)
        square = jnp.sum(squares, axis=-1, keepdims=True)
        if first:
            refs[1][rows] = square
            continue
        rest = lax.rsqrt((refs[0][rows] + square) / DIM + EPS)
        lane = lax.broadcasted_iota(jnp.int32, (SHARD, EXTRA), 1)
        tail = jnp.zeros((SHARD, EXTRA), jnp.float32)
        for i in range(3):
            term = rest.astype(jnp.bfloat16).astype(jnp.float32)
            tail = jnp.where(lane == i, term, tail)
            rest = rest - term
        out_ref[rows, HALF:] = tail.astype(jnp.bfloat16)


def weigh_rows(states, back, gain, earlier):
    whole = pl.BlockSpec(memory_space=pltpu.VMEM)
    first = earlier is None
    out_shape = [jax.ShapeDtypeStruct((ROWS, HALF + (0 if first else EXTRA)), jnp.bfloat16)]
    if first:
        out_shape.append(jax.ShapeDtypeStruct((ROWS, 1), jnp.float32))
    operands = [*states, back, gain] + ([] if first else [earlier])
    return pl.pallas_call(
        functools.partial(weigh_kernel, first),
        out_shape=out_shape,
        in_specs=[whole] * len(operands),
        out_specs=[whole] * len(out_shape),
        compiler_params=pltpu.CompilerParams(vmem_limit_bytes=16 * MEBI),
        cost_estimate=pl.CostEstimate(
            flops=6 * ROWS * HALF, bytes_accessed=8 * ROWS * HALF, transcendentals=0
        ),
    )(*operands)


def ordered(piece):
    rows = []
    for t in range(STEPS):
        at = slice(t * SHARD, (t + 1) * SHARD)
        rows += [piece(i, at) for i in range(NZ)]
    return jnp.concatenate(rows, axis=0)


def times(weight, rows):
    return lax.dot_general(
        weight, rows, (((1,), (1,)), ((), ())), preferred_element_type=jnp.float32
    )


def first_kernel(weight_ref, *refs):
    near = NZ - 1
    low_refs, high_refs = refs[:near], refs[near : 2 * near]
    total, weight_out, high_out, low, sems = refs[2 * near :]
    waiting = []
    for part in range(HALF // PART):
        at = slice(part * PART, (part + 1) * PART)
        pairs = [(weight_ref.at[:, at], weight_out.at[:, at])]
        pairs += [(ref.at[:, at], low.at[i, :, at]) for i, ref in enumerate(low_refs)]
        waiting.append(copies(pairs, sems.at[part]))
    pairs = [(weight_ref.at[:, HALF:], weight_out.at[:, HALF:])]
    pairs += [(ref, high_out.at[i]) for i, ref in enumerate(high_refs)]
    waiting.append(copies(pairs, sems.at[HALF // PART]))
    for part in range(HALF // PART):
        for copy in waiting[part]:
            copy.wait()
        at = slice(part * PART, (part + 1) * PART)
        nothing = jnp.zeros((SHARD, PART), jnp.bfloat16)
        rows = ordered(lambda i, rows: low[i, rows, at] if i < near else nothing)
        product = times(weight_out[:, at], rows)
        if part == 0:
            total[...] = product
        else:
            total[...] += product
    for copy in waiting[-1]:
        copy.wait()


def project_first(weight, low, high):
    near = NZ - 1
    lanes = STEPS * LANES
    operands = [pltpu.with_memory_space_constraint(x, pltpu.HBM) for x in (weight, *low, *high)]
    return pl.pallas_call(
        first_kernel,
        out_shape=[
            jax.ShapeDtypeStruct((NY * COLS, lanes), jnp.float32),
            jax.ShapeDtypeStruct(weight.shape, jnp.bfloat16),
            jax.ShapeDtypeStruct((near, ROWS, HALF + EXTRA), jnp.bfloat16),
        ],
        in_specs=[pl.BlockSpec(memory_space=pltpu.HBM)] * len(operands),
        out_specs=[pl.BlockSpec(memory_space=pltpu.VMEM)] * 3,
        scratch_shapes=[
            pltpu.VMEM((near, ROWS, HALF), jnp.bfloat16),
            pltpu.SemaphoreType.DMA((HALF // PART + 1, NZ)),
        ],
        compiler_params=pltpu.CompilerParams(vmem_limit_bytes=VMEM_PROJECT),
        cost_estimate=pl.CostEstimate(
            flops=2 * NY * COLS * HALF * lanes,
            bytes_accessed=2 * DIM * (NY * COLS + 2 * NZ * ROWS),
            transcendentals=0,
        ),
    )(*operands)


def second_kernel(weight_ref, far_ref, carried_ref, total_ref):
    rows = jnp.concatenate(
        [far_ref[...], jnp.zeros((LANES - ROWS, HALF), jnp.bfloat16)], axis=0
    )
    product = times(weight_ref[:, :HALF], rows)
    lane = lax.broadcasted_iota(jnp.int32, product.shape, 1)
    for t in range(STEPS):
        at = slice(t * LANES, (t + 1) * LANES)
        moved = pltpu.roll(product, LANES - SHARD - t * SHARD, 1)
        total_ref[:, at] = carried_ref[:, at] + jnp.where(lane >= LANES - SHARD, moved, 0.0)


def project_second(weight, far, carried):
    whole = pl.BlockSpec(memory_space=pltpu.VMEM)
    return pl.pallas_call(
        second_kernel,
        out_shape=jax.ShapeDtypeStruct(carried.shape, jnp.float32),
        in_specs=[whole] * 3,
        out_specs=whole,
        compiler_params=pltpu.CompilerParams(vmem_limit_bytes=VMEM_PROJECT),
        cost_estimate=pl.CostEstimate(
            flops=2 * NY * COLS * HALF * LANES,
            bytes_accessed=2 * HALF * NY * COLS,
            transcendentals=0,
        ),
    )(weight, far, carried)


def last_kernel(place_ref, weight_ref, near_ref, far_ref, carried, cos_ref, sin_ref, *refs):
    *outs, total = refs

    def part(first, width):
        at = slice(first, first + width)
        return ordered(
            lambda i, rows: near_ref[i, rows, at] if i < NZ - 1 else far_ref[rows, at]
        )

    for first in range(0, HALF, PART):
        at = HALF + first
        product = times(weight_ref[:, at : at + PART], part(first, PART))
        total[...] = (carried if first == 0 else total)[...] + product
    ones = jnp.where(lax.broadcasted_iota(jnp.int32, (8, EXTRA), 1) < 3, 1.0, 0.0)
    scale = times(ones.astype(jnp.bfloat16), part(HALF, EXTRA))[0:1]
    y = place_ref[1]

    for by in range(NY):
        to = lax.rem(y + by, NY)
        kv_rows = pl.ds(pl.multiple_of(to * KV, KV), KV)
        low = to * COLS
        high = low + SIDE

        def result(base, offset, rows):
            return total[pl.ds(pl.multiple_of(base + offset, KV), rows), :] * scale

        def put(offset, value):
            outs[by][offset : offset + value.shape[0], :] = value.astype(jnp.bfloat16)

        a, b = result(low, Q, KV), result(high, Q, KV)
        cosine, sine = cos_ref[kv_rows, :], sin_ref[kv_rows, :]
        put(0, a * cosine - b * sine)
        put(KV, b * cosine + a * sine)
        put(2 * KV, result(low, Q + KV, KV))
        put(3 * KV, result(high, Q + KV, KV))
        a, b = result(low, 0, Q), result(high, 0, Q)
        cosine, sine = cos_ref[...], sin_ref[...]
        put(4 * KV, a * cosine - b * sine)
        put(4 * KV + Q, b * cosine + a * sine)


def project_last(place, weight, near, far, carried, cosine, sine):
    lanes = STEPS * LANES
    whole = pl.BlockSpec(memory_space=pltpu.VMEM)
    return pl.pallas_call(
        last_kernel,
        out_shape=[jax.ShapeDtypeStruct((COLS, lanes), jnp.bfloat16)] * NY,
        in_specs=[pl.BlockSpec(memory_space=pltpu.SMEM)] + [whole] * 6,
        out_specs=[whole] * NY,
        scratch_shapes=[pltpu.VMEM((NY * COLS, lanes), jnp.float32)],
        compiler_params=pltpu.CompilerParams(vmem_limit_bytes=VMEM_PROJECT),
        cost_estimate=pl.CostEstimate(
            flops=2 * NY * COLS * HALF * lanes,
            bytes_accessed=2 * HALF * (NY * COLS + lanes),
            transcendentals=0,
        ),
    )(place, weight, near, far, carried, cosine, sine)


def chosen_kernel(place_ref, out_ref):
    y, z = place_ref[1], place_ref[2]
    width = NZ * NY * SHARD
    lane = lax.broadcasted_iota(jnp.int32, (LANES, 1), 0)
    column = lax.broadcasted_iota(jnp.int32, (LANES, width), 1)
    group = lane // SHARD
    distance = jnp.zeros((LANES, 1), jnp.int32)
    for i, d in enumerate(ORDER):
        distance = jnp.where(group == i, d, distance)
    plane = lax.rem(z + NZ - distance, NZ)
    for by in range(NY):
        source = lax.rem(y + NY - by, NY)
        at = plane * (NY * SHARD) + source * SHARD + lane % SHARD
        chosen = jnp.where(at == column, 1.0, 0.0).astype(jnp.bfloat16)
        out_ref[by * LANES : (by + 1) * LANES, :] = chosen


def choose_places(place):
    return pl.pallas_call(
        chosen_kernel,
        out_shape=jax.ShapeDtypeStruct((NY * LANES, NZ * NY * SHARD), jnp.bfloat16),
        in_specs=[pl.BlockSpec(memory_space=pltpu.SMEM)],
        out_specs=pl.BlockSpec(memory_space=pltpu.VMEM),
    )(place)


def place_kernel(chosen_ref, *refs):
    pieces, (keys, values, queries) = refs[:NY], refs[NY:]
    width = NZ * NY * SHARD
    for t in range(STEPS):
        lanes = slice(t * LANES, (t + 1) * LANES)
        full = jnp.dot(
            jnp.concatenate([ref[:, lanes] for ref in pieces], axis=1),
            chosen_ref[...],
            preferred_element_type=jnp.float32,
        ).astype(jnp.bfloat16)
        keys[t, 0] = full[: 2 * KV].reshape(2, KV, width)
        values[t, 0] = full[2 * KV : 4 * KV].reshape(2, KV, width)
        queries[t, 0] = full[4 * KV :].reshape(2, Q, width)


def place_outputs(chosen, pieces):
    width = NZ * NY * SHARD
    whole = pl.BlockSpec(memory_space=pltpu.VMEM)
    return pl.pallas_call(
        place_kernel,
        out_shape=[
            jax.ShapeDtypeStruct((STEPS, 1, 2, KV, width), jnp.bfloat16),
            jax.ShapeDtypeStruct((STEPS, 1, 2, KV, width), jnp.bfloat16),
            jax.ShapeDtypeStruct((STEPS, 1, 2, Q, width), jnp.bfloat16),
        ],
        in_specs=[whole] * (1 + len(pieces)),
        out_specs=[whole] * 3,
        compiler_params=pltpu.CompilerParams(vmem_limit_bytes=16 * MEBI),
    )(chosen, *pieces)


def after(value, *earlier):
    return lax.optimization_barrier((value, *earlier))[0]


def on_device(hidden, exits, lengths, norm_gain, w_key, w_value, w_query):
    core = lax.axis_index("dp").astype(jnp.int32)
    layer = lax.axis_index("section").astype(jnp.int32)
    index = lax.axis_index("tensor").astype(jnp.int32)
    z, y = index // NY, index % NY
    place = jnp.stack([core, y, z])

    code = lax.dynamic_slice_in_dim(exits, index * SHARD, SHARD, axis=1)
    depth = jnp.where(code == 1, 1, jnp.where(code == 2, 2, 4))
    back = (layer - jnp.minimum(depth, layer)).reshape(ROWS, 1)

    everyone = jnp.arange(lengths.shape[0], dtype=jnp.int32)
    pair = jnp.arange(HEAD // 2, dtype=jnp.int32).astype(jnp.float32)
    freqs = THETA ** (-(pair * 2.0) / HEAD)

    def tables(planes):
        delta = jnp.array(list(planes), dtype=jnp.int32)
        rows = ((z + NZ - delta) % NZ) * (NY * SHARD) + y * SHARD
        rows = (rows[:, None] + jnp.arange(SHARD, dtype=jnp.int32)[None, :]).reshape(-1)
        mine = jnp.sum(jnp.where(rows[:, None] == everyone[None, :], lengths[None, :], 0), axis=1)
        positions = mine[None, :] + jnp.arange(STEPS, dtype=jnp.int32)[:, None]
        angles = freqs[:, None] * positions.reshape(-1).astype(jnp.float32)[None, :]
        return jnp.cos(angles), jnp.sin(angles)

    *own, half = split(place, hidden.reshape(ROWS, DIM), w_query, w_key, w_value)

    weight = lax.all_gather(
        half, ("dp", "tensor"), axis_index_groups=WEIGHT_GROUPS, tiled=True
    )

    moved = []
    for mine in own:
        two = lax.ppermute(mine, "section", [(1, 3)])
        one = lax.ppermute(mine, "section", [(1, 2), (2, 3)])
        moved.append((mine, one, two))
    low, square = weigh_rows(moved[0], back, norm_gain[:, :HALF], None)
    (high,) = weigh_rows(moved[1], back, norm_gain[:, HALF:], square)

    early = (*tables(ORDER), choose_places(place))
    chains = []
    for half, rows in enumerate((low, high)):
        up, down = [rows], [rows]
        for hop in range(3):
            here = (up[-1], down[-1])
            if half == 1 and hop == 2:
                *here, cosine, sine, chosen = lax.optimization_barrier((*here, *early))
            else:
                here = lax.optimization_barrier(here)
            up.append(shift_z(here[0], 1))
            down.append(shift_z(here[1], -1))
        here = lax.optimization_barrier((up[-1], down[-1]))
        last = shift_z(after(here[half], weight) if half else here[half], 1 - 2 * half)
        chains.append(up + [last] + down[:0:-1])

    low, high = ([chain[d] for d in ORDER] for chain in chains)
    carried, weight, near = project_first(weight, low[:-1], high[:-1])
    carried = project_second(weight, low[-1], carried)
    outs = project_last(place, weight, near, high[-1], carried, cosine, sine)
    pieces = [outs[0], shift_y(outs[1], 1), shift_y(outs[2], 2), shift_y(outs[3], -1)]
    return tuple(place_outputs(chosen, pieces))


def solution(mesh):
    return jax.shard_map(
        on_device,
        mesh=mesh,
        in_specs=(
            P(None, "section", ("dp", "tensor"), None),
            P(None, "dp"),
            P("dp"),
            P("section", None),
            P("section", None, "tensor", None),
            P("section", None, "tensor", None),
            P("section", None, "tensor", None),
        ),
        out_specs=(
            P(None, "section", None, "tensor", "dp"),
            P(None, "section", None, "tensor", "dp"),
            P(None, "section", None, "tensor", "dp"),
        ),
        check_vma=False,
    )
```

```python
import functools

import jax
import jax.numpy as jnp
from jax import lax
from jax.experimental import pallas as pl
from jax.experimental.pallas import tpu as pltpu
from jax.sharding import PartitionSpec as P

HEAD = 128
EPS = 1e-05
THETA = 10000.0

STEPS = 3
DIM = 8192
HALF = DIM // 2
SHARD = 16
NZ = 8
NY = 4
KV = 16
Q = 64
SIDE = Q + 2 * KV
COLS = 2 * SIDE
ROWS = STEPS * SHARD
LANES = NZ * SHARD
PARTS = 2
PART = DIM // PARTS
STEP = 1024
MEBI = 1024 * 1024
VMEM_PROJECT = 16 * MEBI
TILE = 128
HIGH_ROWS = ROWS * (HALF // TILE) + SHARD
ORDER = (0, 1, 2, 3, 5, 6, 7, 4)
CHUNK = 512
WEIGHT_GROUPS = [
    [core * NZ * NY + z * NY + y for y in range(NY) for core in range(2)] for z in range(NZ)
]


def shift_z(value, by):
    pairs = [(z * NY + y, ((z + by) % NZ) * NY + y) for z in range(NZ) for y in range(NY)]
    return lax.ppermute(value, "tensor", pairs)


def shift_y(value, by):
    pairs = [(z * NY + y, z * NY + (y + by) % NY) for z in range(NZ) for y in range(NY)]
    return lax.ppermute(value, "tensor", pairs)


def copies(pairs, sems):
    started = []
    for i, (source, target) in enumerate(pairs):
        copy = pltpu.make_async_copy(source, target, sems.at[i])
        copy.start()
        started.append(copy)
    return started


def split_kernel(place_ref, rows_ref, query_ref, key_ref, value_ref, low_ref, high_ref, half_ref):
    k = pl.program_id(0)
    steps = pl.num_programs(0) // 2

    @pl.when(k < steps)
    def _():
        low_ref[...] = rows_ref[...]

    @pl.when(k >= steps)
    def _():
        high_ref[...] = rows_ref[...]

    half_ref[:Q] = query_ref[0, 0]
    half_ref[Q : Q + KV] = key_ref[0, 0]
    half_ref[Q + KV :] = value_ref[0, 0]


def split(place, rows, query, key, value):
    steps = 1

    def mine(count):
        return pl.BlockSpec((1, 1, count, HALF), lambda k, p: (0, p[0], 0, k))

    return pl.pallas_call(
        split_kernel,
        out_shape=[
            jax.ShapeDtypeStruct((ROWS, HALF), jnp.bfloat16),
            jax.ShapeDtypeStruct((ROWS, HALF), jnp.bfloat16),
            jax.ShapeDtypeStruct((SIDE, DIM), jnp.bfloat16),
        ],
        grid_spec=pltpu.PrefetchScalarGridSpec(
            num_scalar_prefetch=1,
            grid=(2 * steps,),
            in_specs=[
                pl.BlockSpec((ROWS, HALF), lambda k, p: (0, k)),
                mine(Q),
                mine(KV),
                mine(KV),
            ],
            out_specs=[
                pl.BlockSpec((ROWS, HALF), lambda k, p: (0, jnp.minimum(k, steps - 1))),
                pl.BlockSpec((ROWS, HALF), lambda k, p: (0, jnp.maximum(k - steps, 0))),
                pl.BlockSpec((SIDE, HALF), lambda k, p: (0, k)),
            ],
        ),
        compiler_params=pltpu.CompilerParams(vmem_limit_bytes=16 * MEBI),
        cost_estimate=pl.CostEstimate(
            flops=0, bytes_accessed=4 * (ROWS + SIDE) * DIM, transcendentals=0
        ),
    )(place, *(pltpu.with_memory_space_constraint(x, pltpu.HBM) for x in (rows, query, key, value)))


def weigh_kernel(first, own_ref, two_ref, one_ref, back_ref, gain_ref, *refs):
    out_ref = refs[0] if first else refs[1]
    lane = lax.broadcasted_iota(jnp.int32, (SHARD, TILE), 1)
    scales = jnp.zeros((SHARD, TILE), jnp.float32)
    for t in range(STEPS):
        rows = slice(t * SHARD, (t + 1) * SHARD)
        back = back_ref[rows]
        squares = jnp.zeros((SHARD, CHUNK), jnp.float32)
        for start in range(0, HALF, CHUNK):
            at = slice(start, start + CHUNK)
            own, one, two = (ref[rows, at].astype(jnp.float32) for ref in (own_ref, one_ref, two_ref))
            wide = jnp.where(back == 2, two, jnp.where(back == 1, one, own))
            squares += wide * wide
            weighed = (wide * gain_ref[:, at].astype(jnp.float32)).astype(jnp.bfloat16)
            if first:
                out_ref[rows, at] = weighed
                continue
            for column in range(0, CHUNK, TILE):
                target = (start + column) // TILE * ROWS + t * SHARD
                out_ref[target : target + SHARD, :] = weighed[:, column : column + TILE]
        square = jnp.sum(squares, axis=-1, keepdims=True)
        if first:
            refs[1][rows] = square
            continue
        rest = lax.rsqrt((refs[0][rows] + square) / DIM + EPS)
        for i in range(3):
            term = rest.astype(jnp.bfloat16).astype(jnp.float32)
            scales = jnp.where(lane == 3 * t + i, term, scales)
            rest = rest - term
    if not first:
        out_ref[HIGH_ROWS - SHARD :, :] = scales.astype(jnp.bfloat16)


def weigh_rows(states, back, gain, earlier):
    whole = pl.BlockSpec(memory_space=pltpu.VMEM)
    first = earlier is None
    shape = (ROWS, HALF) if first else (HIGH_ROWS, TILE)
    out_shape = [jax.ShapeDtypeStruct(shape, jnp.bfloat16)]
    if first:
        out_shape.append(jax.ShapeDtypeStruct((ROWS, 1), jnp.float32))
    operands = [*states, back, gain] + ([] if first else [earlier])
    return pl.pallas_call(
        functools.partial(weigh_kernel, first),
        out_shape=out_shape,
        in_specs=[whole] * len(operands),
        out_specs=[whole] * len(out_shape),
        compiler_params=pltpu.CompilerParams(vmem_limit_bytes=16 * MEBI),
        cost_estimate=pl.CostEstimate(
            flops=6 * ROWS * HALF, bytes_accessed=8 * ROWS * HALF, transcendentals=0
        ),
    )(*operands)


def ordered(piece):
    rows = []
    for t in range(STEPS):
        at = slice(t * SHARD, (t + 1) * SHARD)
        rows += [piece(i, at) for i in range(NZ)]
    return jnp.concatenate(rows, axis=0)


def times(weight, rows):
    return lax.dot_general(
        weight, rows, (((1,), (1,)), ((), ())), preferred_element_type=jnp.float32
    )


def first_kernel(weight_ref, *refs):
    near = NZ - 1
    low_refs, high_refs = refs[:near], refs[near : 2 * near]
    total, weight_out, high_out, low, sems = refs[2 * near :]
    waiting = []
    for part in range(HALF // STEP):
        at = slice(part * STEP, (part + 1) * STEP)
        pairs = [(weight_ref.at[:, at], weight_out.at[:, at])]
        pairs += [(ref.at[:, at], low.at[i, :, at]) for i, ref in enumerate(low_refs)]
        waiting.append(copies(pairs, sems.at[part]))
    pairs = [(weight_ref.at[:, HALF:], weight_out.at[:, HALF:])]
    pairs += [(ref, high_out.at[i]) for i, ref in enumerate(high_refs)]
    waiting.append(copies(pairs, sems.at[HALF // STEP]))
    for part in range(HALF // STEP):
        for copy in waiting[part]:
            copy.wait()
        at = slice(part * STEP, (part + 1) * STEP)
        nothing = jnp.zeros((SHARD, STEP), jnp.bfloat16)
        rows = ordered(lambda i, rows: low[i, rows, at] if i < near else nothing)
        product = times(weight_out[:, at], rows)
        if part == 0:
            total[...] = product
        else:
            total[...] += product
    for copy in waiting[-1]:
        copy.wait()


def project_first(weight, low, high):
    near = NZ - 1
    lanes = STEPS * LANES
    operands = [pltpu.with_memory_space_constraint(x, pltpu.HBM) for x in (weight, *low, *high)]
    return pl.pallas_call(
        first_kernel,
        out_shape=[
            jax.ShapeDtypeStruct((NY * COLS, lanes), jnp.float32),
            jax.ShapeDtypeStruct(weight.shape, jnp.bfloat16),
            jax.ShapeDtypeStruct((near, HIGH_ROWS, TILE), jnp.bfloat16),
        ],
        in_specs=[pl.BlockSpec(memory_space=pltpu.HBM)] * len(operands),
        out_specs=[pl.BlockSpec(memory_space=pltpu.VMEM)] * 3,
        scratch_shapes=[
            pltpu.VMEM((near, ROWS, HALF), jnp.bfloat16),
            pltpu.SemaphoreType.DMA((HALF // STEP + 1, NZ)),
        ],
        compiler_params=pltpu.CompilerParams(vmem_limit_bytes=VMEM_PROJECT),
        cost_estimate=pl.CostEstimate(
            flops=2 * NY * COLS * HALF * lanes,
            bytes_accessed=2 * DIM * (NY * COLS + 2 * NZ * ROWS),
            transcendentals=0,
        ),
    )(*operands)


def second_kernel(weight_ref, far_ref, carried_ref, total_ref):
    rows = jnp.concatenate(
        [far_ref[...], jnp.zeros((LANES - ROWS, HALF), jnp.bfloat16)], axis=0
    )
    product = times(weight_ref[:, :HALF], rows)
    lane = lax.broadcasted_iota(jnp.int32, product.shape, 1)
    for t in range(STEPS):
        at = slice(t * LANES, (t + 1) * LANES)
        moved = pltpu.roll(product, LANES - SHARD - t * SHARD, 1)
        total_ref[:, at] = carried_ref[:, at] + jnp.where(lane >= LANES - SHARD, moved, 0.0)


def project_second(weight, far, carried):
    whole = pl.BlockSpec(memory_space=pltpu.VMEM)
    return pl.pallas_call(
        second_kernel,
        out_shape=jax.ShapeDtypeStruct(carried.shape, jnp.float32),
        in_specs=[whole] * 3,
        out_specs=whole,
        compiler_params=pltpu.CompilerParams(vmem_limit_bytes=VMEM_PROJECT),
        cost_estimate=pl.CostEstimate(
            flops=2 * NY * COLS * HALF * LANES,
            bytes_accessed=2 * HALF * NY * COLS,
            transcendentals=0,
        ),
    )(weight, far, carried)


def last_kernel(place_ref, weight_ref, near_ref, far_ref, carried, cos_ref, sin_ref, *refs):
    *outs, total = refs

    def tile(i, first):
        at = slice(first, first + SHARD)
        return near_ref[i, at] if i < NZ - 1 else far_ref[at]

    def piece(i, rows):
        tiles = [tile(i, column * ROWS + rows.start) for column in range(HALF // TILE)]
        return jnp.concatenate(tiles, axis=1)

    total[...] = carried[...] + times(weight_ref[:, HALF:], ordered(piece))
    scales = jnp.concatenate([tile(i, HIGH_ROWS - SHARD) for i in range(NZ)], axis=0)
    lane = lax.broadcasted_iota(jnp.int32, (8, TILE), 1)
    scale = []
    for t in range(STEPS):
        ones = jnp.where(lane // 3 == t, 1.0, 0.0).astype(jnp.bfloat16)
        scale.append(times(ones, scales)[0:1])
    scale = jnp.concatenate(scale, axis=1)
    y = place_ref[1]

    for by in range(NY):
        to = lax.rem(y + by, NY)
        kv_rows = pl.ds(pl.multiple_of(to * KV, KV), KV)
        low = to * COLS
        high = low + SIDE

        def result(base, offset, rows):
            return total[pl.ds(pl.multiple_of(base + offset, KV), rows), :] * scale

        def put(offset, value):
            outs[by][offset : offset + value.shape[0], :] = value.astype(jnp.bfloat16)

        a, b = result(low, Q, KV), result(high, Q, KV)
        cosine, sine = cos_ref[kv_rows, :], sin_ref[kv_rows, :]
        put(0, a * cosine - b * sine)
        put(KV, b * cosine + a * sine)
        put(2 * KV, result(low, Q + KV, KV))
        put(3 * KV, result(high, Q + KV, KV))
        a, b = result(low, 0, Q), result(high, 0, Q)
        cosine, sine = cos_ref[...], sin_ref[...]
        put(4 * KV, a * cosine - b * sine)
        put(4 * KV + Q, b * cosine + a * sine)


def project_last(place, weight, near, far, carried, cosine, sine):
    lanes = STEPS * LANES
    whole = pl.BlockSpec(memory_space=pltpu.VMEM)
    return pl.pallas_call(
        last_kernel,
        out_shape=[jax.ShapeDtypeStruct((COLS, lanes), jnp.bfloat16)] * NY,
        in_specs=[pl.BlockSpec(memory_space=pltpu.SMEM)] + [whole] * 6,
        out_specs=[whole] * NY,
        scratch_shapes=[pltpu.VMEM((NY * COLS, lanes), jnp.float32)],
        compiler_params=pltpu.CompilerParams(vmem_limit_bytes=VMEM_PROJECT),
        cost_estimate=pl.CostEstimate(
            flops=2 * NY * COLS * HALF * lanes,
            bytes_accessed=2 * HALF * (NY * COLS + lanes),
            transcendentals=0,
        ),
    )(place, weight, near, far, carried, cosine, sine)


def chosen_kernel(place_ref, out_ref):
    y, z = place_ref[1], place_ref[2]
    width = NZ * NY * SHARD
    lane = lax.broadcasted_iota(jnp.int32, (LANES, 1), 0)
    column = lax.broadcasted_iota(jnp.int32, (LANES, width), 1)
    group = lane // SHARD
    distance = jnp.zeros((LANES, 1), jnp.int32)
    for i, d in enumerate(ORDER):
        distance = jnp.where(group == i, d, distance)
    plane = lax.rem(z + NZ - distance, NZ)
    for slot, by in enumerate((0, 2, 1, 3)):
        source = lax.rem(y + NY - by, NY)
        at = plane * (NY * SHARD) + source * SHARD + lane % SHARD
        chosen = jnp.where(at == column, 1.0, 0.0).astype(jnp.bfloat16)
        out_ref[slot * LANES : (slot + 1) * LANES, :] = chosen


def choose_places(place):
    return pl.pallas_call(
        chosen_kernel,
        out_shape=jax.ShapeDtypeStruct((NY * LANES, NZ * NY * SHARD), jnp.bfloat16),
        in_specs=[pl.BlockSpec(memory_space=pltpu.SMEM)],
        out_specs=pl.BlockSpec(memory_space=pltpu.VMEM),
    )(place)


def place_kernel(chosen_ref, *refs):
    pieces, (keys, values, queries) = refs[:NY], refs[NY:]
    width = NZ * NY * SHARD
    for t in range(STEPS):
        lanes = slice(t * LANES, (t + 1) * LANES)
        full = jnp.dot(
            jnp.concatenate([ref[:, lanes] for ref in pieces], axis=1),
            chosen_ref[...],
            preferred_element_type=jnp.float32,
        ).astype(jnp.bfloat16)
        keys[t, 0] = full[: 2 * KV].reshape(2, KV, width)
        values[t, 0] = full[2 * KV : 4 * KV].reshape(2, KV, width)
        queries[t, 0] = full[4 * KV :].reshape(2, Q, width)


def place_outputs(chosen, pieces):
    width = NZ * NY * SHARD
    whole = pl.BlockSpec(memory_space=pltpu.VMEM)
    return pl.pallas_call(
        place_kernel,
        out_shape=[
            jax.ShapeDtypeStruct((STEPS, 1, 2, KV, width), jnp.bfloat16),
            jax.ShapeDtypeStruct((STEPS, 1, 2, KV, width), jnp.bfloat16),
            jax.ShapeDtypeStruct((STEPS, 1, 2, Q, width), jnp.bfloat16),
        ],
        in_specs=[whole] * (1 + len(pieces)),
        out_specs=[whole] * 3,
        compiler_params=pltpu.CompilerParams(vmem_limit_bytes=16 * MEBI),
    )(chosen, *pieces)


def after(value, *earlier):
    return lax.optimization_barrier((value, *earlier))[0]


def on_device(hidden, exits, lengths, norm_gain, w_key, w_value, w_query):
    core = lax.axis_index("dp").astype(jnp.int32)
    layer = lax.axis_index("section").astype(jnp.int32)
    index = lax.axis_index("tensor").astype(jnp.int32)
    z, y = index // NY, index % NY
    place = jnp.stack([core, y, z])

    code = lax.dynamic_slice_in_dim(exits, index * SHARD, SHARD, axis=1)
    depth = jnp.where(code == 1, 1, jnp.where(code == 2, 2, 4))
    back = (layer - jnp.minimum(depth, layer)).reshape(ROWS, 1)

    everyone = jnp.arange(lengths.shape[0], dtype=jnp.int32)
    pair = jnp.arange(HEAD // 2, dtype=jnp.int32).astype(jnp.float32)
    freqs = THETA ** (-(pair * 2.0) / HEAD)

    def tables(planes):
        delta = jnp.array(list(planes), dtype=jnp.int32)
        rows = ((z + NZ - delta) % NZ) * (NY * SHARD) + y * SHARD
        rows = (rows[:, None] + jnp.arange(SHARD, dtype=jnp.int32)[None, :]).reshape(-1)
        mine = jnp.sum(jnp.where(rows[:, None] == everyone[None, :], lengths[None, :], 0), axis=1)
        positions = mine[None, :] + jnp.arange(STEPS, dtype=jnp.int32)[:, None]
        angles = freqs[:, None] * positions.reshape(-1).astype(jnp.float32)[None, :]
        return jnp.cos(angles), jnp.sin(angles)

    *own, half = split(place, hidden.reshape(ROWS, DIM), w_query, w_key, w_value)

    weight = lax.all_gather(
        half, ("dp", "tensor"), axis_index_groups=WEIGHT_GROUPS, tiled=True
    )

    moved = []
    for mine in own:
        two = lax.ppermute(mine, "section", [(1, 3)])
        one = lax.ppermute(mine, "section", [(1, 2), (2, 3)])
        moved.append((mine, two, one))
    low, square = weigh_rows(moved[0], back, norm_gain[:, :HALF], None)
    (high,) = weigh_rows(moved[1], back, norm_gain[:, HALF:], square)

    early = (*tables(ORDER), choose_places(place))
    chains = []
    for half, rows in enumerate((low, high)):
        up, down = [rows], [rows]
        for hop in range(3):
            here = (up[-1], down[-1])
            if half == 1 and hop == 2:
                *here, cosine, sine, chosen = lax.optimization_barrier((*here, *early))
            else:
                here = lax.optimization_barrier(here)
            up.append(shift_z(here[0], 1))
            down.append(shift_z(here[1], -1))
        here = lax.optimization_barrier((up[-1], down[-1]))
        last = shift_z(after(here[half], weight) if half else here[half], 1 - 2 * half)
        chains.append(up + [last] + down[:0:-1])

    low, high = ([chain[d] for d in ORDER] for chain in chains)
    carried, weight, near = project_first(weight, low[:-1], high[:-1])
    carried = project_second(weight, low[-1], carried)
    outs = project_last(place, weight, near, high[-1], carried, cosine, sine)
    pieces = [outs[0], shift_y(outs[2], 2), shift_y(outs[1], 1), shift_y(outs[3], -1)]
    return tuple(place_outputs(chosen, pieces))


def solution(mesh):
    return jax.shard_map(
        on_device,
        mesh=mesh,
        in_specs=(
            P(None, "section", ("dp", "tensor"), None),
            P(None, "dp"),
            P("dp"),
            P("section", None),
            P("section", None, "tensor", None),
            P("section", None, "tensor", None),
            P("section", None, "tensor", None),
        ),
        out_specs=(
            P(None, "section", None, "tensor", "dp"),
            P(None, "section", None, "tensor", "dp"),
            P(None, "section", None, "tensor", "dp"),
        ),
        check_vma=False,
    )
```

```python
import functools

import jax
import jax.numpy as jnp
from jax import lax
from jax.experimental import pallas as pl
from jax.experimental.pallas import tpu as pltpu
from jax.sharding import PartitionSpec as P

HEAD = 128
EPS = 1e-05
THETA = 10000.0

STEPS = 3
DIM = 8192
HALF = DIM // 2
SHARD = 16
NZ = 8
NY = 4
KV = 16
Q = 64
SIDE = Q + 2 * KV
COLS = 2 * SIDE
ROWS = STEPS * SHARD
LANES = NZ * SHARD
PARTS = 2
PART = DIM // PARTS
STEP = 1024
MEBI = 1024 * 1024
VMEM_PROJECT = 16 * MEBI
TILE = 128
HIGH_ROWS = ROWS * (HALF // TILE) + SHARD
ORDER = (0, 1, 2, 3, 5, 6, 7, 4)
CHUNK = 512
WEIGHT_GROUPS = [
    [core * NZ * NY + z * NY + y for y in range(NY) for core in range(2)] for z in range(NZ)
]


def shift_z(value, by):
    pairs = [(z * NY + y, ((z + by) % NZ) * NY + y) for z in range(NZ) for y in range(NY)]
    return lax.ppermute(value, "tensor", pairs)


def shift_y(value, by):
    pairs = [(z * NY + y, z * NY + (y + by) % NY) for z in range(NZ) for y in range(NY)]
    return lax.ppermute(value, "tensor", pairs)


def copies(pairs, sems):
    started = []
    for i, (source, target) in enumerate(pairs):
        copy = pltpu.make_async_copy(source, target, sems.at[i])
        copy.start()
        started.append(copy)
    return started


def split_kernel(place_ref, rows_ref, query_ref, key_ref, value_ref, low_ref, high_ref, half_ref):
    k = pl.program_id(0)
    steps = pl.num_programs(0) // 2

    @pl.when(k < steps)
    def _():
        low_ref[...] = rows_ref[...]

    @pl.when(k >= steps)
    def _():
        high_ref[...] = rows_ref[...]

    half_ref[:Q] = query_ref[0, 0]
    half_ref[Q : Q + KV] = key_ref[0, 0]
    half_ref[Q + KV :] = value_ref[0, 0]


def split(place, rows, query, key, value):
    steps = 1

    def mine(count):
        return pl.BlockSpec((1, 1, count, HALF), lambda k, p: (0, p[0], 0, k))

    return pl.pallas_call(
        split_kernel,
        out_shape=[
            jax.ShapeDtypeStruct((ROWS, HALF), jnp.bfloat16),
            jax.ShapeDtypeStruct((ROWS, HALF), jnp.bfloat16),
            jax.ShapeDtypeStruct((SIDE, DIM), jnp.bfloat16),
        ],
        grid_spec=pltpu.PrefetchScalarGridSpec(
            num_scalar_prefetch=1,
            grid=(2 * steps,),
            in_specs=[
                pl.BlockSpec((ROWS, HALF), lambda k, p: (0, k)),
                mine(Q),
                mine(KV),
                mine(KV),
            ],
            out_specs=[
                pl.BlockSpec((ROWS, HALF), lambda k, p: (0, jnp.minimum(k, steps - 1))),
                pl.BlockSpec((ROWS, HALF), lambda k, p: (0, jnp.maximum(k - steps, 0))),
                pl.BlockSpec((SIDE, HALF), lambda k, p: (0, k)),
            ],
        ),
        compiler_params=pltpu.CompilerParams(vmem_limit_bytes=16 * MEBI),
        cost_estimate=pl.CostEstimate(
            flops=0, bytes_accessed=4 * (ROWS + SIDE) * DIM, transcendentals=0
        ),
    )(place, *(pltpu.with_memory_space_constraint(x, pltpu.HBM) for x in (rows, query, key, value)))


def weigh_kernel(first, own_ref, two_ref, one_ref, back_ref, gain_ref, *refs):
    out_ref = refs[0] if first else refs[1]
    lane = lax.broadcasted_iota(jnp.int32, (SHARD, TILE), 1)
    scales = jnp.zeros((SHARD, TILE), jnp.float32)
    for t in range(STEPS):
        rows = slice(t * SHARD, (t + 1) * SHARD)
        back = back_ref[rows]
        squares = jnp.zeros((SHARD, CHUNK), jnp.float32)
        for start in range(0, HALF, CHUNK):
            at = slice(start, start + CHUNK)
            own, one, two = (ref[rows, at].astype(jnp.float32) for ref in (own_ref, one_ref, two_ref))
            wide = jnp.where(back == 2, two, jnp.where(back == 1, one, own))
            squares += wide * wide
            weighed = (wide * gain_ref[:, at].astype(jnp.float32)).astype(jnp.bfloat16)
            if first:
                out_ref[rows, at] = weighed
                continue
            for column in range(0, CHUNK, TILE):
                target = (start + column) // TILE * ROWS + t * SHARD
                out_ref[target : target + SHARD, :] = weighed[:, column : column + TILE]
        square = jnp.sum(squares, axis=-1, keepdims=True)
        if first:
            refs[1][rows] = square
            continue
        rest = lax.rsqrt((refs[0][rows] + square) / DIM + EPS)
        for i in range(3):
            term = rest.astype(jnp.bfloat16).astype(jnp.float32)
            scales = jnp.where(lane == 3 * t + i, term, scales)
            rest = rest - term
    if not first:
        out_ref[HIGH_ROWS - SHARD :, :] = scales.astype(jnp.bfloat16)


def weigh_rows(states, back, gain, earlier):
    whole = pl.BlockSpec(memory_space=pltpu.VMEM)
    first = earlier is None
    shape = (ROWS, HALF) if first else (HIGH_ROWS, TILE)
    out_shape = [jax.ShapeDtypeStruct(shape, jnp.bfloat16)]
    if first:
        out_shape.append(jax.ShapeDtypeStruct((ROWS, 1), jnp.float32))
    operands = [*states, back, gain] + ([] if first else [earlier])
    return pl.pallas_call(
        functools.partial(weigh_kernel, first),
        out_shape=out_shape,
        in_specs=[whole] * len(operands),
        out_specs=[whole] * len(out_shape),
        compiler_params=pltpu.CompilerParams(vmem_limit_bytes=16 * MEBI),
        cost_estimate=pl.CostEstimate(
            flops=6 * ROWS * HALF, bytes_accessed=8 * ROWS * HALF, transcendentals=0
        ),
    )(*operands)


def ordered(piece):
    rows = []
    for t in range(STEPS):
        at = slice(t * SHARD, (t + 1) * SHARD)
        rows += [piece(i, at) for i in range(NZ)]
    return jnp.concatenate(rows, axis=0)


def times(weight, rows):
    return lax.dot_general(
        weight, rows, (((1,), (1,)), ((), ())), preferred_element_type=jnp.float32
    )


def first_kernel(weight_ref, *refs):
    near = NZ - 1
    low_refs, high_refs = refs[:near], refs[near : 2 * near]
    total, weight_out, high_out, low, sems = refs[2 * near :]
    waiting = []
    for part in range(HALF // STEP):
        at = slice(part * STEP, (part + 1) * STEP)
        pairs = [(weight_ref.at[:, at], weight_out.at[:, at])]
        pairs += [(ref.at[:, at], low.at[i, :, at]) for i, ref in enumerate(low_refs)]
        waiting.append(copies(pairs, sems.at[part]))
    pairs = [(weight_ref.at[:, HALF:], weight_out.at[:, HALF:])]
    pairs += [(ref, high_out.at[i]) for i, ref in enumerate(high_refs)]
    waiting.append(copies(pairs, sems.at[HALF // STEP]))
    for part in range(HALF // STEP):
        for copy in waiting[part]:
            copy.wait()
        at = slice(part * STEP, (part + 1) * STEP)
        nothing = jnp.zeros((SHARD, STEP), jnp.bfloat16)
        rows = ordered(lambda i, rows: low[i, rows, at] if i < near else nothing)
        product = times(weight_out[:, at], rows)
        if part == 0:
            total[...] = product
        else:
            total[...] += product
    for copy in waiting[-1]:
        copy.wait()


def project_first(weight, low, high):
    near = NZ - 1
    lanes = STEPS * LANES
    fixed = [pltpu.with_memory_space_constraint(x, pltpu.HBM) for x in (weight, *low, *high)]
    operands = [high[i - near - 1] if i == near + 4 else x for i, x in enumerate(fixed)]
    return pl.pallas_call(
        first_kernel,
        out_shape=[
            jax.ShapeDtypeStruct((NY * COLS, lanes), jnp.float32),
            jax.ShapeDtypeStruct(weight.shape, jnp.bfloat16),
            jax.ShapeDtypeStruct((near, HIGH_ROWS, TILE), jnp.bfloat16),
        ],
        in_specs=[
            pl.BlockSpec(memory_space=pl.ANY if i == near + 4 else pltpu.HBM)
            for i in range(len(operands))
        ],
        out_specs=[pl.BlockSpec(memory_space=pltpu.VMEM)] * 3,
        scratch_shapes=[
            pltpu.VMEM((near, ROWS, HALF), jnp.bfloat16),
            pltpu.SemaphoreType.DMA((HALF // STEP + 1, NZ)),
        ],
        compiler_params=pltpu.CompilerParams(vmem_limit_bytes=VMEM_PROJECT),
        cost_estimate=pl.CostEstimate(
            flops=2 * NY * COLS * HALF * lanes,
            bytes_accessed=2 * DIM * (NY * COLS + 2 * NZ * ROWS),
            transcendentals=0,
        ),
    )(*operands)


def second_kernel(weight_ref, far_ref, carried_ref, total_ref):
    rows = jnp.concatenate(
        [far_ref[...], jnp.zeros((LANES - ROWS, HALF), jnp.bfloat16)], axis=0
    )
    product = times(weight_ref[:, :HALF], rows)
    lane = lax.broadcasted_iota(jnp.int32, product.shape, 1)
    for t in range(STEPS):
        at = slice(t * LANES, (t + 1) * LANES)
        moved = pltpu.roll(product, LANES - SHARD - t * SHARD, 1)
        total_ref[:, at] = carried_ref[:, at] + jnp.where(lane >= LANES - SHARD, moved, 0.0)


def project_second(weight, far, carried):
    whole = pl.BlockSpec(memory_space=pltpu.VMEM)
    return pl.pallas_call(
        second_kernel,
        out_shape=jax.ShapeDtypeStruct(carried.shape, jnp.float32),
        in_specs=[whole] * 3,
        out_specs=whole,
        compiler_params=pltpu.CompilerParams(vmem_limit_bytes=VMEM_PROJECT),
        cost_estimate=pl.CostEstimate(
            flops=2 * NY * COLS * HALF * LANES,
            bytes_accessed=2 * HALF * NY * COLS,
            transcendentals=0,
        ),
    )(weight, far, carried)


def last_kernel(place_ref, weight_ref, near_ref, far_ref, carried, cos_ref, sin_ref, *refs):
    *outs, total = refs

    def tile(i, first):
        at = slice(first, first + SHARD)
        return near_ref[i, at] if i < NZ - 1 else far_ref[at]

    def piece(i, rows):
        tiles = [tile(i, column * ROWS + rows.start) for column in range(HALF // TILE)]
        return jnp.concatenate(tiles, axis=1)

    total[...] = carried[...] + times(weight_ref[:, HALF:], ordered(piece))
    scales = jnp.concatenate([tile(i, HIGH_ROWS - SHARD) for i in range(NZ)], axis=0)
    lane = lax.broadcasted_iota(jnp.int32, (8, TILE), 1)
    scale = []
    for t in range(STEPS):
        ones = jnp.where(lane // 3 == t, 1.0, 0.0).astype(jnp.bfloat16)
        scale.append(times(ones, scales)[0:1])
    scale = jnp.concatenate(scale, axis=1)
    y = place_ref[1]

    for by in range(NY):
        to = lax.rem(y + by, NY)
        kv_rows = pl.ds(pl.multiple_of(to * KV, KV), KV)
        low = to * COLS
        high = low + SIDE

        def result(base, offset, rows):
            return total[pl.ds(pl.multiple_of(base + offset, KV), rows), :] * scale

        def put(offset, value):
            outs[by][offset : offset + value.shape[0], :] = value.astype(jnp.bfloat16)

        a, b = result(low, Q, KV), result(high, Q, KV)
        cosine, sine = cos_ref[kv_rows, :], sin_ref[kv_rows, :]
        put(0, a * cosine - b * sine)
        put(KV, b * cosine + a * sine)
        put(2 * KV, result(low, Q + KV, KV))
        put(3 * KV, result(high, Q + KV, KV))
        a, b = result(low, 0, Q), result(high, 0, Q)
        cosine, sine = cos_ref[...], sin_ref[...]
        put(4 * KV, a * cosine - b * sine)
        put(4 * KV + Q, b * cosine + a * sine)


def project_last(place, weight, near, far, carried, cosine, sine):
    lanes = STEPS * LANES
    whole = pl.BlockSpec(memory_space=pltpu.VMEM)
    return pl.pallas_call(
        last_kernel,
        out_shape=[jax.ShapeDtypeStruct((COLS, lanes), jnp.bfloat16)] * NY,
        in_specs=[pl.BlockSpec(memory_space=pltpu.SMEM)] + [whole] * 6,
        out_specs=[whole] * NY,
        scratch_shapes=[pltpu.VMEM((NY * COLS, lanes), jnp.float32)],
        compiler_params=pltpu.CompilerParams(vmem_limit_bytes=VMEM_PROJECT),
        cost_estimate=pl.CostEstimate(
            flops=2 * NY * COLS * HALF * lanes,
            bytes_accessed=2 * HALF * (NY * COLS + lanes),
            transcendentals=0,
        ),
    )(place, weight, near, far, carried, cosine, sine)


def chosen_kernel(place_ref, out_ref):
    y, z = place_ref[1], place_ref[2]
    width = NZ * NY * SHARD
    lane = lax.broadcasted_iota(jnp.int32, (LANES, 1), 0)
    column = lax.broadcasted_iota(jnp.int32, (LANES, width), 1)
    group = lane // SHARD
    distance = jnp.zeros((LANES, 1), jnp.int32)
    for i, d in enumerate(ORDER):
        distance = jnp.where(group == i, d, distance)
    plane = lax.rem(z + NZ - distance, NZ)
    for slot, by in enumerate((0, 2, 1, 3)):
        source = lax.rem(y + NY - by, NY)
        at = plane * (NY * SHARD) + source * SHARD + lane % SHARD
        chosen = jnp.where(at == column, 1.0, 0.0).astype(jnp.bfloat16)
        out_ref[slot * LANES : (slot + 1) * LANES, :] = chosen


def choose_places(place):
    return pl.pallas_call(
        chosen_kernel,
        out_shape=jax.ShapeDtypeStruct((NY * LANES, NZ * NY * SHARD), jnp.bfloat16),
        in_specs=[pl.BlockSpec(memory_space=pltpu.SMEM)],
        out_specs=pl.BlockSpec(memory_space=pltpu.VMEM),
    )(place)


def place_kernel(chosen_ref, *refs):
    pieces, (keys, values, queries) = refs[:NY], refs[NY:]
    width = NZ * NY * SHARD
    for t in range(STEPS):
        lanes = slice(t * LANES, (t + 1) * LANES)
        full = jnp.dot(
            jnp.concatenate([ref[:, lanes] for ref in pieces], axis=1),
            chosen_ref[...],
            preferred_element_type=jnp.float32,
        ).astype(jnp.bfloat16)
        keys[t, 0] = full[: 2 * KV].reshape(2, KV, width)
        values[t, 0] = full[2 * KV : 4 * KV].reshape(2, KV, width)
        queries[t, 0] = full[4 * KV :].reshape(2, Q, width)


def place_outputs(chosen, pieces):
    width = NZ * NY * SHARD
    whole = pl.BlockSpec(memory_space=pltpu.VMEM)
    return pl.pallas_call(
        place_kernel,
        out_shape=[
            jax.ShapeDtypeStruct((STEPS, 1, 2, KV, width), jnp.bfloat16),
            jax.ShapeDtypeStruct((STEPS, 1, 2, KV, width), jnp.bfloat16),
            jax.ShapeDtypeStruct((STEPS, 1, 2, Q, width), jnp.bfloat16),
        ],
        in_specs=[whole] * (1 + len(pieces)),
        out_specs=[whole] * 3,
        compiler_params=pltpu.CompilerParams(vmem_limit_bytes=16 * MEBI),
    )(chosen, *pieces)


def after(value, *earlier):
    return lax.optimization_barrier((value, *earlier))[0]


def on_device(hidden, exits, lengths, norm_gain, w_key, w_value, w_query):
    core = lax.axis_index("dp").astype(jnp.int32)
    layer = lax.axis_index("section").astype(jnp.int32)
    index = lax.axis_index("tensor").astype(jnp.int32)
    z, y = index // NY, index % NY
    place = jnp.stack([core, y, z])

    code = lax.dynamic_slice_in_dim(exits, index * SHARD, SHARD, axis=1)
    depth = jnp.where(code == 1, 1, jnp.where(code == 2, 2, 4))
    back = (layer - jnp.minimum(depth, layer)).reshape(ROWS, 1)

    everyone = jnp.arange(lengths.shape[0], dtype=jnp.int32)
    pair = jnp.arange(HEAD // 2, dtype=jnp.int32).astype(jnp.float32)
    freqs = THETA ** (-(pair * 2.0) / HEAD)

    def tables(planes):
        delta = jnp.array(list(planes), dtype=jnp.int32)
        rows = ((z + NZ - delta) % NZ) * (NY * SHARD) + y * SHARD
        rows = (rows[:, None] + jnp.arange(SHARD, dtype=jnp.int32)[None, :]).reshape(-1)
        mine = jnp.sum(jnp.where(rows[:, None] == everyone[None, :], lengths[None, :], 0), axis=1)
        positions = mine[None, :] + jnp.arange(STEPS, dtype=jnp.int32)[:, None]
        angles = freqs[:, None] * positions.reshape(-1).astype(jnp.float32)[None, :]
        return jnp.cos(angles), jnp.sin(angles)

    *own, half = split(place, hidden.reshape(ROWS, DIM), w_query, w_key, w_value)

    weight = lax.all_gather(
        half, ("dp", "tensor"), axis_index_groups=WEIGHT_GROUPS, tiled=True
    )

    moved = []
    for mine in own:
        two = lax.ppermute(mine, "section", [(1, 3)])
        one = lax.ppermute(mine, "section", [(1, 2), (2, 3)])
        moved.append((mine, two, one))
    low, square = weigh_rows(moved[0], back, norm_gain[:, :HALF], None)
    (high,) = weigh_rows(moved[1], back, norm_gain[:, HALF:], square)

    early = (*tables(ORDER), choose_places(place))
    chains = []
    for half, rows in enumerate((low, high)):
        up, down = [rows], [rows]
        for hop in range(3):
            here = (up[-1], down[-1])
            if half == 1 and hop == 2:
                *here, cosine, sine, chosen = lax.optimization_barrier((*here, *early))
            else:
                here = lax.optimization_barrier(here)
            up.append(shift_z(here[0], 1))
            down.append(shift_z(here[1], -1))
        here = lax.optimization_barrier((up[-1], down[-1]))
        last = shift_z(after(here[half], weight) if half else here[half], 1 - 2 * half)
        chains.append(up + [last] + down[:0:-1])

    low, high = ([chain[d] for d in ORDER] for chain in chains)
    carried, weight, near = project_first(weight, low[:-1], high[:-1])
    carried = project_second(weight, low[-1], carried)
    outs = project_last(place, weight, near, high[-1], carried, cosine, sine)
    pieces = [outs[0], shift_y(outs[2], 2), shift_y(outs[1], 1), shift_y(outs[3], -1)]
    return tuple(place_outputs(chosen, pieces))


def solution(mesh):
    return jax.shard_map(
        on_device,
        mesh=mesh,
        in_specs=(
            P(None, "section", ("dp", "tensor"), None),
            P(None, "dp"),
            P("dp"),
            P("section", None),
            P("section", None, "tensor", None),
            P("section", None, "tensor", None),
            P("section", None, "tensor", None),
        ),
        out_specs=(
            P(None, "section", None, "tensor", "dp"),
            P(None, "section", None, "tensor", "dp"),
            P(None, "section", None, "tensor", "dp"),
        ),
        check_vma=False,
    )
```
